1024 devices in a mesh: blk: 256 (over y, z_lo, x), group: 4 (over z_hi, core).
Axes of the slice: x: 4, y: 8, z: 16 (z_hi: 2, z_lo: 8; z = z_hi * 8 + z_lo), core: 2. Of those that a mesh axis runs over, the one named last changes fastest.
Arguments:
- image: bfloat16 [131072, 1152], P(('blk', 'group')), may hold values from -0.1796875 to 0.1796875
- text: bfloat16 [131072, 1152], P(('blk', 'group')), may hold values from -0.1796875 to 0.1796875
- positives: int32 [131072], P(('blk', 'group')), may hold values from 0 to 127, as said below
- logit_scale: float32 [1], replicated, may hold values from 4 to 16
- logit_bias: float32 [1], replicated, may hold values from -4 to -1
Outputs:
- image_grad: float32 [131072, 1152], P(('blk', 'group'))
- text_grad: float32 [131072, 1152], P(('blk', 'group'))
The draws below stay inside these ranges and needn't reach their ends.
Inputs may be any that keep to these rules, and one draw needn't show every extreme that they name: `positives`: each aligned block of 128 entries is a permutation of 0 to 127.
All inputs are finite; a program needn't handle non-finite values.
Results may differ from the reference program's by a relative error of at most 0.004.
Values may be sent and summed in bfloat16 or wider, within the bound.
No kernel may reach another device: no remote copies, remote signals or barrier semaphores. Data moves between devices by JAX's collectives and lax.ppermute only.
A program may use at most 32 MiB of HBM per device.

```python
import math
import jax
import jax.numpy as jnp
from jax import lax

D = 1152
ROWS = 128
ROUNDS = 2
TOTAL = 131072
N_BLK = 256
N_GROUP = 4


def draw_positives(key, part):
    key = jax.random.fold_in(key, 11)
    block_keys = jax.random.split(key, TOTAL // ROWS)
    perms = jax.vmap(lambda one_key: jax.random.permutation(one_key, ROWS))(block_keys)
    return perms.reshape(TOTAL).astype(jnp.int32)


def block_scale(stream_key, dims, pieces, smallest, high):
    gain, own = 1.0, jax.random.fold_in(stream_key, 6)
    for position, parts in pieces:
        steps = jnp.exp(jax.random.uniform(jax.random.fold_in(own, position), (parts,), jnp.float32, smallest / len(pieces), high / len(pieces)))
        gain = gain * jnp.repeat(steps, dims[position] // parts).reshape([-1 if axis == position else 1 for axis in range(len(dims))])
    return gain


def scatter_about(own_key, extent, spread, reach, pieces=(), kind=jnp.bfloat16):
    entries = spread * jax.random.normal(own_key, extent, jnp.float32)
    if pieces:
        entries = entries * block_scale(own_key, extent, pieces, -0.22, 0.18)
    return jnp.clip(entries, -reach, reach).astype(kind)


def setup_inputs(seed: int = 0) -> dict:
    key_of = jax.random.split(jax.random.key(seed), 6)
    image = scatter_about(key_of[0], (TOTAL, D), 0.03, 0.1796875, ((0, 1024),))
    text = scatter_about(key_of[1], (TOTAL, D), 0.03, 0.1796875, ((0, 1024),))
    positives = draw_positives(jax.random.fold_in(key_of[5], 71), 0)
    logit_scale = jnp.clip(jnp.exp(jax.random.uniform(key_of[3], (1,), jnp.float32, math.log(4.0), math.log(16.0))), 4.0, 16.0)
    logit_bias = jnp.clip(jax.random.uniform(key_of[4], (1,), jnp.float32, -4.0, -1.0), -4.0, -1.0)
    return dict(image=image, text=text, positives=positives, logit_scale=logit_scale, logit_bias=logit_bias)


norm_eps = 1e-06

def unit_rows(values):
    wide = values.astype(jnp.float32)
    inverse = lax.rsqrt(lax.optimization_barrier(jnp.sum(wide * wide, axis=-1, keepdims=True)) + norm_eps)
    return (wide, inverse, (wide * inverse).astype(jnp.bfloat16))

def unit_backward(wide, inverse, upstream):
    inner = lax.optimization_barrier(jnp.sum(wide * upstream, axis=-1, keepdims=True))
    return inverse * (upstream - inverse * inverse * wide * inner)

def reference(image, text, positives, logit_scale, logit_bias):
    image_wide, image_inv, image_unit = unit_rows(image)
    text_wide, text_inv, text_unit = unit_rows(text)
    image_blocks = image_unit.reshape(N_BLK, N_GROUP, ROWS, D)
    text_blocks = text_unit.reshape(N_BLK, N_GROUP, ROWS, D)
    pos_blocks = positives.reshape(N_BLK, N_GROUP, ROWS)
    logit_mult = logit_scale[0]
    logit_add = logit_bias[0]
    image_acc = jnp.zeros((N_BLK, N_GROUP, ROWS, D), jnp.float32)
    text_acc = jnp.zeros((N_BLK, N_GROUP, ROWS, D), jnp.float32)
    for turn_index in range(ROUNDS):
        met_text = jnp.roll(text_blocks, turn_index, axis=0)

        def tile_terms(tile_items):
            image_tile, text_tile, pos_tile = tile_items
            image_f = image_tile.astype(jnp.float32)
            text_f = text_tile.astype(jnp.float32)
            logits = logit_mult * jnp.einsum('gid,hjd->ghij', image_f, text_f) + logit_add
            weights = jax.nn.sigmoid(logits)
            if turn_index == 0:
                column_ids = jnp.arange(ROWS, dtype=jnp.int32)
                hit = column_ids[None, None, None, :] == pos_tile[:, None, :, None]
                same_group = jnp.eye(N_GROUP, dtype=bool)[:, :, None, None]
                weights = weights - (hit & same_group).astype(jnp.float32)
            coeff = lax.optimization_barrier(weights.astype(jnp.bfloat16)).astype(jnp.float32)
            image_term = logit_mult * jnp.einsum('ghij,hjd->gid', coeff, text_f)
            text_term = logit_mult * jnp.einsum('ghij,gid->hjd', coeff, image_f)
            return (image_term, text_term)
        image_part, text_part = lax.map(tile_terms, (image_blocks, met_text, pos_blocks))
        image_acc = image_acc + image_part
        text_acc = text_acc + jnp.roll(text_part, -turn_index, axis=0)
    image_grad = unit_backward(image_wide, image_inv, image_acc.reshape(TOTAL, D))
    text_grad = unit_backward(text_wide, text_inv, text_acc.reshape(TOTAL, D))
    return (image_grad, text_grad)
```

```python
import functools
import jax
import jax.numpy as jnp
from jax import lax
from jax.experimental import pallas as pl
from jax.experimental.pallas import tpu as pltpu
from jax.sharding import PartitionSpec as P

AXES = ("blk", "group")
norm_eps = 1e-06


def moved(value, steps, flip):
    blocks, groups = lax.axis_size("blk"), lax.axis_size("group")
    pairs = [
        (b * groups + g, ((b + steps) % blocks) * groups + (g ^ flip))
        for b in range(blocks)
        for g in range(groups)
    ]
    return lax.ppermute(value, AXES, pairs)


def unit_rows(values):
    wide = values.astype(jnp.float32)
    inverse = lax.rsqrt(jnp.sum(wide * wide, axis=-1, keepdims=True) + norm_eps)
    return (wide, inverse, (wide * inverse).astype(jnp.bfloat16))


def unit_backward(wide, inverse, upstream):
    inner = jnp.sum(wide * upstream, axis=-1, keepdims=True)
    return inverse * (upstream - inverse * inverse * wide * inner)


def dot_rows(a, b):
    return lax.dot_general(a, b, (((1,), (1,)), ((), ())), preferred_element_type=jnp.float32)


def gradient_terms(count, diagonal, final, *refs):
    scale_ref, bias_ref, image_ref, text_ref = refs[:4]
    refs = refs[4:]
    scale, bias = scale_ref[0], bias_ref[0]
    image_wide, image_inv, image_unit = unit_rows(image_ref[...])
    text_wide, text_inv, text_unit = unit_rows(text_ref[...])
    image_sum = text_sum = None

    def add(total, term):
        return term if total is None else total + term

    if diagonal:
        pos_ref, refs = refs[0], refs[1:]
        weights = jax.nn.sigmoid(scale * dot_rows(image_unit, text_unit) + bias)
        columns = lax.broadcasted_iota(jnp.int32, weights.shape, 1)
        weights = weights - (columns == pos_ref[...]).astype(jnp.float32)
        image_sum = jnp.dot(weights.astype(jnp.bfloat16), text_unit, preferred_element_type=jnp.float32)
        text_sum = jnp.dot(weights.T.astype(jnp.bfloat16), image_unit, preferred_element_type=jnp.float32)
    if not diagonal:
        image_sum, text_sum = refs[0][...], refs[1][...]
        refs = refs[2:]
    text_refs, image_refs, outs = refs[: count[0]], refs[count[0] : sum(count)], refs[sum(count) :]
    for met_ref in text_refs:
        met = unit_rows(met_ref[...])[2]
        weights = jax.nn.sigmoid(scale * dot_rows(image_unit, met) + bias)
        image_sum = image_sum + jnp.dot(weights.astype(jnp.bfloat16), met, preferred_element_type=jnp.float32)
    for met_ref in image_refs:
        met = unit_rows(met_ref[...])[2]
        weights = jax.nn.sigmoid(scale * dot_rows(text_unit, met) + bias)
        text_sum = text_sum + jnp.dot(weights.astype(jnp.bfloat16), met, preferred_element_type=jnp.float32)
    if final:
        image_sum = unit_backward(image_wide, image_inv, scale * image_sum)
        text_sum = unit_backward(text_wide, text_inv, scale * text_sum)
    outs[0][...] = image_sum
    outs[1][...] = text_sum


def terms(scale, bias, image, text, met_texts, met_images, positives=None, sums=None, final=False):
    smem = pl.BlockSpec(memory_space=pltpu.SMEM)
    vmem = pl.BlockSpec(memory_space=pltpu.VMEM)
    diagonal = positives is not None
    extra = [positives[:, None]] if diagonal else list(sums)
    operands = [image, text, *extra, *met_texts, *met_images]
    rows, width = image.shape
    out = jax.ShapeDtypeStruct((rows, width), jnp.float32)
    subs = len(met_texts) + len(met_images)
    return pl.pallas_call(
        functools.partial(gradient_terms, (len(met_texts), len(met_images)), diagonal, final),
        out_shape=(out, out),
        in_specs=[smem, smem] + [vmem] * len(operands),
        out_specs=(vmem, vmem),
        compiler_params=pltpu.CompilerParams(vmem_limit_bytes=40 * 1024 * 1024),
        cost_estimate=pl.CostEstimate(
            flops=4 * rows * rows * width * subs, bytes_accessed=2 * rows * width * (subs + 6), transcendentals=0
        ),
    )(scale, bias, *operands)


def local(image, text, positives, scale, bias):
    far_text = moved(text, 0, 2)
    far_image = moved(image, 0, 2)
    last_text = moved(text, 1, 0)
    next_image = moved(image, -1, 0)
    near = [text, last_text, image, next_image]
    twin = [moved(v, 0, 1) for v in near]
    sums = terms(
        scale, bias, image, text, [twin[0], last_text, twin[1]], [twin[2], next_image, twin[3]], positives=positives
    )
    far_last_text = moved(far_text, 1, 0)
    far_next_image = moved(far_image, -1, 0)
    far_text_twin = moved(far_text, 0, 1)
    far_image_twin = moved(far_image, 0, 1)
    sums = terms(scale, bias, image, text, [far_text, far_text_twin], [far_image, far_image_twin], sums=sums)
    far_last_twin = moved(far_last_text, 0, 1)
    far_next_twin = moved(far_next_image, 0, 1)
    return terms(
        scale,
        bias,
        image,
        text,
        [far_last_text, far_last_twin],
        [far_next_image, far_next_twin],
        sums=sums,
        final=True,
    )


def solution(mesh):
    in_specs = (P(AXES, None), P(AXES, None), P(AXES), P(), P())
    out_specs = (P(AXES, None), P(AXES, None))
    return jax.shard_map(local, mesh=mesh, in_specs=in_specs, out_specs=out_specs, check_vma=False)
```

```python
import functools
import jax
import jax.numpy as jnp
from jax import lax
from jax.experimental import pallas as pl
from jax.experimental.pallas import tpu as pltpu
from jax.sharding import PartitionSpec as P

AXES = ("blk", "group")
norm_eps = 1e-06


def moved(value, steps, flip):
    blocks, groups = lax.axis_size("blk"), lax.axis_size("group")
    pairs = [
        (b * groups + g, ((b + steps) % blocks) * groups + (g ^ flip))
        for b in range(blocks)
        for g in range(groups)
    ]
    return lax.ppermute(value, AXES, pairs)


def unit_rows(values):
    wide = values.astype(jnp.float32)
    inverse = lax.rsqrt(jnp.sum(wide * wide, axis=-1, keepdims=True) + norm_eps)
    return (wide, inverse, (wide * inverse).astype(jnp.bfloat16))


def unit_backward(wide, inverse, upstream):
    inner = jnp.sum(wide * upstream, axis=-1, keepdims=True)
    return inverse * (upstream - inverse * inverse * wide * inner)


def dot_rows(a, b):
    return lax.dot_general(a, b, (((1,), (1,)), ((), ())), preferred_element_type=jnp.float32)


def gradient_terms(count, diagonal, final, *refs):
    scale_ref, bias_ref, image_ref, text_ref = refs[:4]
    refs = refs[4:]
    scale, bias = scale_ref[0], bias_ref[0]
    image_wide, image_inv, image_unit = unit_rows(image_ref[...])
    text_wide, text_inv, text_unit = unit_rows(text_ref[...])
    image_sum = text_sum = None

    def add(total, term):
        return term if total is None else total + term

    if diagonal:
        pos_ref, refs = refs[0], refs[1:]
        weights = jax.nn.sigmoid(scale * dot_rows(image_unit, text_unit) + bias)
        columns = lax.broadcasted_iota(jnp.int32, weights.shape, 1)
        weights = weights - (columns == pos_ref[...]).astype(jnp.float32)
        image_sum = jnp.dot(weights.astype(jnp.bfloat16), text_unit, preferred_element_type=jnp.float32)
        text_sum = jnp.dot(weights.T.astype(jnp.bfloat16), image_unit, preferred_element_type=jnp.float32)
    if not diagonal:
        image_sum, text_sum = refs[0][...], refs[1][...]
        refs = refs[2:]
    rows = image_ref.shape[0]
    texts, images, both = count
    text_blocks = [(ref, 0) for ref in refs[:texts]]
    image_blocks = [(ref, 0) for ref in refs[texts : texts + images]]
    text_blocks += [(ref, 0) for ref in refs[texts + images : sum(count)]]
    image_blocks += [(ref, rows) for ref in refs[texts + images : sum(count)]]
    outs = refs[sum(count) :]
    for met_ref, start in text_blocks:
        met = unit_rows(met_ref[pl.ds(start, rows), :])[2]
        weights = jax.nn.sigmoid(scale * dot_rows(image_unit, met) + bias)
        image_sum = image_sum + jnp.dot(weights.astype(jnp.bfloat16), met, preferred_element_type=jnp.float32)
    for met_ref, start in image_blocks:
        met = unit_rows(met_ref[pl.ds(start, rows), :])[2]
        weights = jax.nn.sigmoid(scale * dot_rows(text_unit, met) + bias)
        text_sum = text_sum + jnp.dot(weights.astype(jnp.bfloat16), met, preferred_element_type=jnp.float32)
    if final:
        image_sum = unit_backward(image_wide, image_inv, scale * image_sum)
        text_sum = unit_backward(text_wide, text_inv, scale * text_sum)
    outs[0][...] = image_sum
    outs[1][...] = text_sum


def terms(scale, bias, image, text, met_texts, met_images, met_both, positives=None, sums=None, final=False):
    smem = pl.BlockSpec(memory_space=pltpu.SMEM)
    vmem = pl.BlockSpec(memory_space=pltpu.VMEM)
    diagonal = positives is not None
    extra = [positives[:, None]] if diagonal else list(sums)
    operands = [image, text, *extra, *met_texts, *met_images, *met_both]
    rows, width = image.shape
    out = jax.ShapeDtypeStruct((rows, width), jnp.float32)
    subs = len(met_texts) + len(met_images) + 2 * len(met_both)
    return pl.pallas_call(
        functools.partial(gradient_terms, (len(met_texts), len(met_images), len(met_both)), diagonal, final),
        out_shape=(out, out),
        in_specs=[smem, smem] + [vmem] * len(operands),
        out_specs=(vmem, vmem),
        compiler_params=pltpu.CompilerParams(vmem_limit_bytes=40 * 1024 * 1024),
        cost_estimate=pl.CostEstimate(
            flops=4 * rows * rows * width * subs, bytes_accessed=2 * rows * width * (subs + 6), transcendentals=0
        ),
    )(scale, bias, *operands)


RUN = 32


def moved_block(value, steps):
    blocks, groups = lax.axis_size("blk"), lax.axis_size("group")
    pairs = []
    for b in range(blocks):
        to = (b + steps) % blocks
        flip = 0 if b // RUN == to // RUN else groups // 2
        pairs += [(b * groups + g, to * groups + (g ^ flip)) for g in range(groups)]
    return lax.ppermute(value, AXES, pairs)


def moved_half(value):
    return moved(value, 0, lax.axis_size("group") // 2)


def moved_core(value):
    return moved(value, 0, 1)


def local(image, text, positives, scale, bias):
    rows = text.shape[0]
    own = jnp.concatenate([text, image])
    far = moved_half(own)
    last_text = moved_block(text, 1)
    next_image = moved_block(image, -1)
    twin = moved_core(own)
    sums = terms(scale, bias, image, text, [], [], [twin], positives=positives)
    far, last_text, next_image, sums = lax.optimization_barrier((far, last_text, next_image, sums))
    far_last_text = moved_block(far[:rows], 1)
    far_next_image = moved_block(far[rows:], -1)
    far_twin = moved_core(far)
    moved_twin = moved_core(jnp.concatenate([last_text, next_image]))
    sums = terms(scale, bias, image, text, [last_text], [next_image], [far, far_twin, moved_twin], sums=sums)
    far_moved_twin = moved_core(jnp.concatenate([far_last_text, far_next_image]))
    return terms(
        scale, bias, image, text, [far_last_text], [far_next_image], [far_moved_twin], sums=sums, final=True
    )


def solution(mesh):
    in_specs = (P(AXES, None), P(AXES, None), P(AXES), P(), P())
    out_specs = (P(AXES, None), P(AXES, None))
    return jax.shard_map(local, mesh=mesh, in_specs=in_specs, out_specs=out_specs, check_vma=False)
```

```python
import functools
import jax
import jax.numpy as jnp
from jax import lax
from jax.experimental import pallas as pl
from jax.experimental.pallas import tpu as pltpu
from jax.sharding import PartitionSpec as P

AXES = ("blk", "group")
norm_eps = 1e-06
RUN = 32
ROWS = 128
WEIGHT = 40


def moved_block(value, steps):
    blocks, groups = lax.axis_size("blk"), lax.axis_size("group")
    pairs = []
    for b in range(blocks):
        to = (b + steps) % blocks
        flip = 0 if b // RUN == to // RUN else groups // 2
        pairs += [(b * groups + g, to * groups + (g ^ flip)) for g in range(groups)]
    return lax.ppermute(value, AXES, pairs)


def moved_group(value, flip):
    blocks, groups = lax.axis_size("blk"), lax.axis_size("group")
    pairs = [(b * groups + g, b * groups + (g ^ flip)) for b in range(blocks) for g in range(groups)]
    return lax.ppermute(value, AXES, pairs)


def moved_half(value):
    return moved_group(value, lax.axis_size("group") // 2)


def moved_core(value):
    return moved_group(value, 1)


def unit_rows(values):
    wide = values.astype(jnp.float32)
    inverse = lax.rsqrt(jnp.sum(wide * wide, axis=-1, keepdims=True) + norm_eps)
    return (wide, inverse, (wide * inverse).astype(jnp.bfloat16))


def unit_backward(wide, inverse, upstream):
    inner = jnp.sum(wide * upstream, axis=-1, keepdims=True)
    return inverse * (upstream - inverse * inverse * wide * inner)


def dot_rows(a, b):
    return lax.dot_general(a, b, (((1,), (1,)), ((), ())), preferred_element_type=jnp.float32)


def dot_sum(coeff, unit):
    return jnp.dot(coeff.astype(jnp.bfloat16), unit, preferred_element_type=jnp.float32)


def add_met(total, scale, bias, unit, met_refs):
    rows = unit.shape[0]
    for ref, start in met_refs:
        met = unit_rows(ref[pl.ds(start, rows), :])[2]
        term = dot_sum(jax.nn.sigmoid(scale * dot_rows(unit, met) + bias), met)
        total = total + term
    return total


def first_kernel(texts, images, count, scale_ref, bias_ref, image_ref, text_ref, pos_ref, *refs):
    met, (image_out, text_out) = refs[:count], refs[count:]
    scale, bias = scale_ref[0], bias_ref[0]
    image_unit = unit_rows(image_ref[...])[2]
    text_unit = unit_rows(text_ref[...])[2]
    weights = jax.nn.sigmoid(scale * dot_rows(image_unit, text_unit) + bias)
    columns = lax.broadcasted_iota(jnp.int32, weights.shape, 1)
    weights = weights - (columns == pos_ref[...]).astype(jnp.float32)
    image_sum, text_sum = dot_sum(weights, text_unit), dot_sum(weights.T, image_unit)
    image_out[...] = add_met(image_sum, scale, bias, image_unit, [(met[k], s) for k, s in texts])
    text_out[...] = add_met(text_sum, scale, bias, text_unit, [(met[k], s) for k, s in images])


def next_kernel(jobs, count, scale_ref, bias_ref, *refs):
    met, refs = refs[:count], refs[count:]
    scale, bias = scale_ref[0], bias_ref[0]
    outs = refs[2 * len(jobs) :]
    for job, (places, final) in enumerate(jobs):
        wide, inverse, unit = unit_rows(refs[2 * job][...])
        total = add_met(refs[2 * job + 1][...], scale, bias, unit, [(met[k], s) for k, s in places])
        outs[job][...] = unit_backward(wide, inverse, scale * total) if final else total


SMEM = pl.BlockSpec(memory_space=pltpu.SMEM)
VMEM = pl.BlockSpec(memory_space=pltpu.VMEM)


def call(body, scalars, operands, outs, terms):
    width = operands[0].shape[1]
    out = jax.ShapeDtypeStruct((ROWS, width), jnp.float32)
    return pl.pallas_call(
        body,
        out_shape=(out,) * outs,
        in_specs=[SMEM] * 2 + [VMEM] * len(operands),
        out_specs=(VMEM,) * outs,
        compiler_params=pltpu.CompilerParams(vmem_limit_bytes=40 * 1024 * 1024),
        cost_estimate=pl.CostEstimate(
            flops=WEIGHT * 4 * ROWS * ROWS * width * terms,
            bytes_accessed=2 * ROWS * width * (terms + 4 * outs),
            transcendentals=ROWS * ROWS * terms,
        ),
    )(*scalars, *operands)


def first_terms(scalars, image, text, positives, met, texts, images):
    body = functools.partial(first_kernel, texts, images, len(met))
    return call(body, scalars, [image, text, positives[:, None], *met], 2, 2 + len(texts) + len(images))


def next_terms(scalars, met, *jobs):
    body = functools.partial(next_kernel, [job[2:] for job in jobs], len(met))
    own = [array for job in jobs for array in job[:2]]
    return call(body, scalars, [*met, *own], len(jobs), sum(len(job[2]) for job in jobs))


def local(image, text, positives, scale, bias):
    scalars = (scale, bias)
    far_text = moved_half(text)
    far_image = moved_half(image)
    last_text = moved_block(text, 1)
    next_image = moved_block(image, -1)
    twin = moved_core(jnp.concatenate([text, image]))
    sums = first_terms(scalars, image, text, positives, [twin], [(0, 0)], [(0, ROWS)])
    far_last_text = moved_block(far_text, 1)
    mid_twin = moved_core(jnp.concatenate([far_text, last_text, next_image]))
    far_next_image = moved_block(far_image, -1)
    image_sum, text_sum = next_terms(scalars, [far_text, last_text, next_image, mid_twin], (image, sums[0], [(0, 0), (1, 0), (3, 0), (3, ROWS)], False), (text, sums[1], [(2, 0), (3, 2 * ROWS)], False))
    late_twin = moved_core(jnp.concatenate([far_last_text, far_image]))
    image_grad, text_sum = next_terms(scalars, [far_last_text, far_image, late_twin], (image, image_sum, [(0, 0), (2, 0)], True), (text, text_sum, [(1, 0), (2, ROWS)], False))
    far_next_image, text_sum = lax.optimization_barrier((far_next_image, text_sum))
    last_twin = moved_core(far_next_image)
    (text_grad,) = next_terms(scalars, [far_next_image, last_twin], (text, text_sum, [(0, 0), (1, 0)], True))
    return (image_grad, text_grad)


def solution(mesh):
    in_specs = (P(AXES, None), P(AXES, None), P(AXES), P(), P())
    out_specs = (P(AXES, None), P(AXES, None))
    return jax.shard_map(local, mesh=mesh, in_specs=in_specs, out_specs=out_specs, check_vma=False)
```

```python
import functools
import jax
import jax.numpy as jnp
from jax import lax
from jax.experimental import pallas as pl
from jax.experimental.pallas import tpu as pltpu
from jax.sharding import PartitionSpec as P

AXES = ("blk", "group")
norm_eps = 1e-06
RUN = 32
ROWS = 128
WEIGHTS = (40, 40, 40, 40)


def moved_block(value, steps):
    blocks, groups = lax.axis_size("blk"), lax.axis_size("group")
    pairs = []
    for b in range(blocks):
        to = (b + steps) % blocks
        flip = 0 if b // RUN == to // RUN else groups // 2
        pairs += [(b * groups + g, to * groups + (g ^ flip)) for g in range(groups)]
    return lax.ppermute(value, AXES, pairs)


def moved_group(value, flip):
    blocks, groups = lax.axis_size("blk"), lax.axis_size("group")
    pairs = [(b * groups + g, b * groups + (g ^ flip)) for b in range(blocks) for g in range(groups)]
    return lax.ppermute(value, AXES, pairs)


def moved_half(value):
    return moved_group(value, lax.axis_size("group") // 2)


def moved_core(value):
    return moved_group(value, 1)


def unit_rows(values):
    wide = values.astype(jnp.float32)
    inverse = lax.rsqrt(jnp.sum(wide * wide, axis=-1, keepdims=True) + norm_eps)
    return (wide, inverse, (wide * inverse).astype(jnp.bfloat16))


def unit_backward(wide, inverse, upstream):
    inner = jnp.sum(wide * upstream, axis=-1, keepdims=True)
    return inverse * (upstream - inverse * inverse * wide * inner)


def dot_rows(a, b):
    return lax.dot_general(a, b, (((1,), (1,)), ((), ())), preferred_element_type=jnp.float32)


def dot_sum(coeff, unit):
    return jnp.dot(coeff.astype(jnp.bfloat16), unit, preferred_element_type=jnp.float32)


def add_met(total, scale, bias, unit, met_refs):
    rows = unit.shape[0]
    met = jnp.concatenate([unit_rows(ref[pl.ds(start, rows), :])[2] for ref, start in met_refs])
    return total + dot_sum(jax.nn.sigmoid(scale * dot_rows(unit, met) + bias), met)


def first_kernel(texts, images, count, scale_ref, bias_ref, image_ref, text_ref, pos_ref, *refs):
    met, (image_out, text_out) = refs[:count], refs[count:]
    scale, bias = scale_ref[0], bias_ref[0]
    image_unit = unit_rows(image_ref[...])[2]
    text_unit = unit_rows(text_ref[...])[2]
    weights = jax.nn.sigmoid(scale * dot_rows(image_unit, text_unit) + bias)
    columns = lax.broadcasted_iota(jnp.int32, weights.shape, 1)
    weights = weights - (columns == pos_ref[...]).astype(jnp.float32)
    image_sum, text_sum = dot_sum(weights, text_unit), dot_sum(weights.T, image_unit)
    image_out[...] = add_met(image_sum, scale, bias, image_unit, [(met[k], s) for k, s in texts])
    text_out[...] = add_met(text_sum, scale, bias, text_unit, [(met[k], s) for k, s in images])


def next_kernel(jobs, count, scale_ref, bias_ref, *refs):
    met, refs = refs[:count], refs[count:]
    scale, bias = scale_ref[0], bias_ref[0]
    outs = refs[2 * len(jobs) :]
    for job, (places, final) in enumerate(jobs):
        wide, inverse, unit = unit_rows(refs[2 * job][...])
        total = add_met(refs[2 * job + 1][...], scale, bias, unit, [(met[k], s) for k, s in places])
        outs[job][...] = unit_backward(wide, inverse, scale * total) if final else total


SMEM = pl.BlockSpec(memory_space=pltpu.SMEM)
VMEM = pl.BlockSpec(memory_space=pltpu.VMEM)


def call(turn, body, scalars, operands, outs, terms):
    width = operands[0].shape[1]
    out = jax.ShapeDtypeStruct((ROWS, width), jnp.float32)
    return pl.pallas_call(
        body,
        out_shape=(out,) * outs,
        in_specs=[SMEM] * 2 + [VMEM] * len(operands),
        out_specs=(VMEM,) * outs,
        compiler_params=pltpu.CompilerParams(vmem_limit_bytes=40 * 1024 * 1024),
        cost_estimate=pl.CostEstimate(
            flops=WEIGHTS[turn] * 4 * ROWS * ROWS * width * terms,
            bytes_accessed=2 * ROWS * width * (terms + 4 * outs),
            transcendentals=ROWS * ROWS * terms,
        ),
    )(*scalars, *operands)


def first_terms(scalars, image, text, positives, met, texts, images):
    body = functools.partial(first_kernel, texts, images, len(met))
    return call(0, body, scalars, [image, text, positives[:, None], *met], 2, 2 + len(texts) + len(images))


def next_terms(turn, scalars, met, *jobs):
    body = functools.partial(next_kernel, [job[2:] for job in jobs], len(met))
    own = [array for job in jobs for array in job[:2]]
    return call(turn, body, scalars, [*met, *own], len(jobs), sum(len(job[2]) for job in jobs))


def local(image, text, positives, scale, bias):
    scalars = (scale, bias)
    far_text = moved_half(text)
    far_image = moved_half(image)
    last_text = moved_block(text, 1)
    next_image = moved_block(image, -1)
    twin = moved_core(jnp.concatenate([text, image]))
    sums = first_terms(scalars, image, text, positives, [twin], [(0, 0)], [(0, ROWS)])
    far_last_text = moved_block(far_text, 1)
    mid_twin = moved_core(jnp.concatenate([far_text, last_text, next_image]))
    sums = next_terms(
        1,
        scalars,
        [far_text, last_text, next_image, mid_twin],
        (image, sums[0], [(0, 0), (1, 0), (3, 0), (3, ROWS)], False),
        (text, sums[1], [(2, 0), (3, 2 * ROWS)], False),
    )
    far_next_image = moved_block(far_image, -1)
    image_sum, text_sum = sums
    image_twin = moved_core(far_image)
    (text_sum,) = next_terms(2, scalars, [far_image, image_twin], (text, text_sum, [(0, 0), (1, 0)], False))
    last_twin = moved_core(jnp.concatenate([far_last_text, far_next_image]))
    return next_terms(
        3,
        scalars,
        [far_last_text, far_next_image, last_twin],
        (image, image_sum, [(0, 0), (2, 0)], True),
        (text, text_sum, [(1, 0), (2, ROWS)], True),
    )


def solution(mesh):
    in_specs = (P(AXES, None), P(AXES, None), P(AXES), P(), P())
    out_specs = (P(AXES, None), P(AXES, None))
    return jax.shard_map(local, mesh=mesh, in_specs=in_specs, out_specs=out_specs, check_vma=False)
```

```python
import functools
import jax
import jax.numpy as jnp
from jax import lax
from jax.experimental import pallas as pl
from jax.experimental.pallas import tpu as pltpu
from jax.sharding import PartitionSpec as P

AXES = ("blk", "group")
norm_eps = 1e-06
RUN = 32
ROWS = 128
WEIGHTS = (120, 120, 120, 120)


def moved_block(value, steps):
    blocks, groups = lax.axis_size("blk"), lax.axis_size("group")
    pairs = []
    for b in range(blocks):
        to = (b + steps) % blocks
        flip = 0 if b // RUN == to // RUN else groups // 2
        pairs += [(b * groups + g, to * groups + (g ^ flip)) for g in range(groups)]
    return lax.ppermute(value, AXES, pairs)


def moved_group(value, flip):
    blocks, groups = lax.axis_size("blk"), lax.axis_size("group")
    pairs = [(b * groups + g, b * groups + (g ^ flip)) for b in range(blocks) for g in range(groups)]
    return lax.ppermute(value, AXES, pairs)


def moved_half(value):
    return moved_group(value, lax.axis_size("group") // 2)


def moved_core(value):
    return moved_group(value, 1)


def unit_rows(values):
    wide = values.astype(jnp.float32)
    inverse = lax.rsqrt(jnp.sum(wide * wide, axis=-1, keepdims=True) + norm_eps)
    return (wide, inverse, (wide * inverse).astype(jnp.bfloat16))


def unit_backward(wide, inverse, upstream):
    inner = jnp.sum(wide * upstream, axis=-1, keepdims=True)
    return inverse * (upstream - inverse * inverse * wide * inner)


def dot_rows(a, b):
    return lax.dot_general(a, b, (((1,), (1,)), ((), ())), preferred_element_type=jnp.float32)


def dot_sum(coeff, unit):
    return jnp.dot(coeff.astype(jnp.bfloat16), unit, preferred_element_type=jnp.float32)


def add_met(total, scale, bias, unit, met_refs):
    rows = unit.shape[0]
    met = jnp.concatenate([unit_rows(ref[pl.ds(start, rows), :])[2] for ref, start in met_refs])
    return total + dot_sum(jax.nn.sigmoid(scale * dot_rows(unit, met) + bias), met)


def first_kernel(texts, images, count, scale_ref, bias_ref, image_ref, text_ref, pos_ref, *refs):
    met, (image_out, text_out) = refs[:count], refs[count:]
    scale, bias = scale_ref[0], bias_ref[0]
    image_unit = unit_rows(image_ref[...])[2]
    text_unit = unit_rows(text_ref[...])[2]
    weights = jax.nn.sigmoid(scale * dot_rows(image_unit, text_unit) + bias)
    columns = lax.broadcasted_iota(jnp.int32, weights.shape, 1)
    weights = weights - (columns == pos_ref[...]).astype(jnp.float32)
    image_sum, text_sum = dot_sum(weights, text_unit), dot_sum(weights.T, image_unit)
    image_out[...] = add_met(image_sum, scale, bias, image_unit, [(met[k], s) for k, s in texts])
    text_out[...] = add_met(text_sum, scale, bias, text_unit, [(met[k], s) for k, s in images])


def next_kernel(jobs, count, scale_ref, bias_ref, *refs):
    met, refs = refs[:count], refs[count:]
    scale, bias = scale_ref[0], bias_ref[0]
    outs = refs[2 * len(jobs) :]
    for job, (places, final) in enumerate(jobs):
        wide, inverse, unit = unit_rows(refs[2 * job][...])
        total = add_met(refs[2 * job + 1][...], scale, bias, unit, [(met[k], s) for k, s in places])
        outs[job][...] = unit_backward(wide, inverse, scale * total) if final else total


SMEM = pl.BlockSpec(memory_space=pltpu.SMEM)
VMEM = pl.BlockSpec(memory_space=pltpu.VMEM)


def call(turn, body, scalars, operands, outs, terms):
    width = operands[0].shape[1]
    out = jax.ShapeDtypeStruct((ROWS, width), jnp.float32)
    return pl.pallas_call(
        body,
        out_shape=(out,) * outs,
        in_specs=[SMEM] * 2 + [VMEM] * len(operands),
        out_specs=(VMEM,) * outs,
        compiler_params=pltpu.CompilerParams(vmem_limit_bytes=40 * 1024 * 1024),
        cost_estimate=pl.CostEstimate(
            flops=WEIGHTS[turn] * 4 * ROWS * ROWS * width * terms,
            bytes_accessed=2 * ROWS * width * (terms + 4 * outs),
            transcendentals=ROWS * ROWS * terms,
        ),
    )(*scalars, *operands)


def first_terms(scalars, image, text, positives, met, texts, images):
    body = functools.partial(first_kernel, texts, images, len(met))
    return call(0, body, scalars, [image, text, positives[:, None], *met], 2, 2 + len(texts) + len(images))


def next_terms(turn, scalars, met, *jobs):
    body = functools.partial(next_kernel, [job[2:] for job in jobs], len(met))
    own = [array for job in jobs for array in job[:2]]
    return call(turn, body, scalars, [*met, *own], len(jobs), sum(len(job[2]) for job in jobs))


def local(image, text, positives, scale, bias):
    scalars = (scale, bias)
    far_text = moved_half(text)
    far_image = moved_half(image)
    last_text = moved_block(text, 1)
    next_image = moved_block(image, -1)
    twin = moved_core(jnp.concatenate([text, image]))
    far_last_text = moved_block(far_text, 1)
    far_next_image = moved_block(far_image, -1)
    far_twin = moved_core(jnp.concatenate([far_text, far_image]))
    last_twin = moved_core(jnp.concatenate([last_text, far_last_text, next_image, far_next_image]))
    sums = first_terms(scalars, image, text, positives, [twin], [(0, 0)], [(0, ROWS)])
    image_sum, text_sum = next_terms(
        1,
        scalars,
        [far_text, far_image, far_twin, last_text, far_last_text, next_image, far_next_image],
        (image, sums[0], [(0, 0), (2, 0), (3, 0), (4, 0)], False),
        (text, sums[1], [(1, 0), (2, ROWS), (5, 0), (6, 0)], False),
    )
    return next_terms(
        3,
        scalars,
        [last_twin],
        (image, image_sum, [(0, 0), (0, ROWS)], True),
        (text, text_sum, [(0, 2 * ROWS), (0, 3 * ROWS)], True),
    )


def solution(mesh):
    in_specs = (P(AXES, None), P(AXES, None), P(AXES), P(), P())
    out_specs = (P(AXES, None), P(AXES, None))
    return jax.shard_map(local, mesh=mesh, in_specs=in_specs, out_specs=out_specs, check_vma=False)
```
